32 devices in a mesh: dp: 16 (over z, y, x), proto: 2 (over core).
Axes of the slice: x: 2, y: 2, z: 4, core: 2. Of those that a mesh axis runs over, the one named last changes fastest.
Arguments:
- teacher: bfloat16 [4096, 128], P('dp'), may hold values from -1000 to 1000
- student: bfloat16 [4096, 128], P('dp'), may hold values from -1000 to 1000
- prototypes: bfloat16 [128, 65536], P('dp', 'proto'), may hold values from -1 to 1, as said below
Outputs:
- crop_loss: float32 [4096], P('dp')
- logit_grad: bfloat16 [4096, 65536], P('dp', 'proto')
- proto_grad: bfloat16 [128, 65536], P('dp', 'proto')
The draws below stay inside these ranges and needn't reach their ends.
Inputs may be any that keep to these rules, and one draw needn't show every extreme that they name: `prototypes`: prototype columns have unit length.
All inputs are finite; a program needn't handle non-finite values.
Results may differ from the reference program's by a relative error of at most 0.015.
Values may be sent and summed in bfloat16 or wider, within the bound.
No kernel may reach another device: no remote copies, remote signals or barrier semaphores. Data moves between devices by JAX's collectives and lax.ppermute only.
A program may use at most 128 MiB of HBM per device.

```python
import jax
import jax.numpy as jnp
from jax import lax

ROWS = 256
D = 128
K = 65536
ITERS = 3
CROPS = 4096
N_DP = 16


def proto_columns(key):
    normals = jax.random.normal(key, (D, K), jnp.float32)
    return normals / jnp.sqrt(jnp.sum(normals * normals, axis=0, keepdims=True))


def draw_prototypes(key, part):
    columns = proto_columns(key)
    return columns.astype(jnp.bfloat16)


def draw_teacher(key, part):
    key = jax.random.fold_in(key, 11)
    return (4.0 * jax.random.normal(key, (CROPS, D), jnp.float32)).astype(jnp.bfloat16)


def draw_student(key, part):
    key = jax.random.fold_in(key, 23)
    return (3.0 * jax.random.normal(key, (CROPS, D), jnp.float32)).astype(jnp.bfloat16)


def setup_inputs(seed: int = 0) -> dict:
    key_list = jax.random.split(jax.random.key(seed), 4)
    return {
        "teacher": draw_teacher(jax.random.fold_in(key_list[3], 71), 0),
        "student": draw_student(jax.random.fold_in(key_list[3], 71), 0),
        "prototypes": draw_prototypes(jax.random.fold_in(key_list[3], 71), 0),
    }


def block_exp(rows_in, prototypes):
    scores = jnp.dot(rows_in, prototypes, preferred_element_type=jnp.float32)
    return jnp.exp(scores - jnp.max(scores, axis=1, keepdims=True))


def reference(teacher, student, prototypes):
    teacher_blocks = teacher.reshape(N_DP, ROWS, D)
    student_blocks = student.reshape(N_DP, ROWS, D)
    row_scale = lax.map(lambda rows_in: 1.0 / jnp.sum(block_exp(rows_in, prototypes), axis=1), teacher_blocks)
    col_scale = jnp.zeros((K,), jnp.float32)
    for sweep_index in range(ITERS):
        def column_part(pair_in):
            rows_in, scale_in = pair_in
            return jnp.sum(block_exp(rows_in, prototypes) * scale_in[:, None], axis=0)
        col_total = jnp.sum(lax.map(column_part, (teacher_blocks, row_scale)), axis=0)
        col_scale = 1.0 / (K * col_total)

        def row_part(rows_in):
            return 1.0 / (CROPS * jnp.sum(block_exp(rows_in, prototypes) * col_scale[None, :], axis=1))
        row_scale = lax.map(row_part, teacher_blocks)

    def final_block(grad_sum, pair_in):
        teach_in, stud_in, scale_in = pair_in
        targets = CROPS * block_exp(teach_in, prototypes) * scale_in[:, None] * col_scale[None, :]
        scores = jnp.dot(stud_in, prototypes, preferred_element_type=jnp.float32)
        row_peak = jnp.max(scores, axis=1, keepdims=True)
        shifted = jnp.exp(scores - row_peak)
        exp_total = jnp.sum(shifted, axis=1, keepdims=True)
        log_probs = scores - row_peak - jnp.log(exp_total)
        crop_loss = -jnp.sum(targets * log_probs, axis=1)
        logit_grad = (K * (shifted / exp_total - targets)).astype(jnp.bfloat16)
        grad_term = lax.dot_general(stud_in, logit_grad, (((0,), (0,)), ((), ())), preferred_element_type=jnp.float32)
        grad_part = lax.optimization_barrier(grad_term.astype(jnp.bfloat16))
        return grad_sum + grad_part.astype(jnp.float32), (crop_loss, logit_grad)

    grad_sum, (loss_blocks, grad_blocks) = lax.scan(final_block, jnp.zeros((D, K), jnp.float32), (teacher_blocks, student_blocks, row_scale))
    return loss_blocks.reshape(CROPS), grad_blocks.reshape(CROPS, K), (grad_sum / 128.0).astype(jnp.bfloat16)
```

```python
import functools

import jax
import jax.numpy as jnp
from jax import lax
from jax.experimental import pallas as pl
from jax.experimental.pallas import tpu as pltpu
from jax.sharding import PartitionSpec as P

ITERS = 3
F32 = jnp.float32
BF16 = jnp.bfloat16
NT = (((1,), (1,)), ((), ()))


def params(mib=40):
    return pltpu.CompilerParams(
        vmem_limit_bytes=mib * 1024 * 1024, dimension_semantics=("arbitrary",)
    )


def full(shape):
    return pl.BlockSpec(shape, lambda i: (0,) * len(shape))


def split_hi_lo(v):
    hi = v.astype(BF16)
    return hi, (v - hi.astype(F32)).astype(BF16)


def exp_kernel(kc, protos, crops, x_out, peak_out, total_out, protos_t, scores):
    width = protos_t.shape[0]
    rb = crops.shape[0]

    @pl.when(pl.program_id(0) == 0)
    def _():
        for k in range(0, width, 128):
            protos_t[k : k + 128, :] = protos[:, k : k + 128].astype(F32).T.astype(BF16)

    peak = jnp.full((8, rb), -jnp.inf, F32)
    for k in range(0, width, kc):
        s = lax.dot_general(
            protos_t[k : k + kc, :], crops[...], NT, preferred_element_type=F32
        )
        scores[k : k + kc, :] = s
        peak = jnp.maximum(peak, jnp.max(s.reshape(kc // 8, 8, rb), axis=0))
    peak = jnp.max(peak, axis=0, keepdims=True)
    total = jnp.zeros((8, rb), F32)
    for k in range(0, width, kc):
        e = jnp.exp(scores[k : k + kc, :] - peak)
        total = total + jnp.sum(e.reshape(kc // 8, 8, rb), axis=0)
        x_out[k : k + kc, :] = e.astype(BF16)
    peak_out[...] = peak
    total_out[...] = jnp.sum(total, axis=0, keepdims=True)


def exp_rows(protos, crops):
    depth, width = protos.shape
    n = crops.shape[0]
    rb = 512
    kc = min(256, width)
    return pl.pallas_call(
        functools.partial(exp_kernel, kc),
        grid=(n // rb,),
        in_specs=[full((depth, width)), pl.BlockSpec((rb, depth), lambda i: (i, 0))],
        out_specs=[
            pl.BlockSpec((width, rb), lambda i: (0, i)),
            pl.BlockSpec((1, rb), lambda i: (0, i)),
            pl.BlockSpec((1, rb), lambda i: (0, i)),
        ],
        out_shape=[
            jax.ShapeDtypeStruct((width, n), BF16),
            jax.ShapeDtypeStruct((1, n), F32),
            jax.ShapeDtypeStruct((1, n), F32),
        ],
        scratch_shapes=[pltpu.VMEM((width, depth), BF16), pltpu.VMEM((width, rb), F32)],
        compiler_params=params(),
        cost_estimate=pl.CostEstimate(
            flops=2 * n * width * depth, bytes_accessed=2 * n * width, transcendentals=n * width
        ),
        name="exp_rows",
    )(protos, crops)


def sweep_kernel(protos_all, x, weight, factor, part_out, col_out, weights2, acc):
    step = pl.program_id(0)
    kb, n = x.shape

    @pl.when(step == 0)
    def _():
        hi, lo = split_hi_lo(weight[...])
        row = lax.broadcasted_iota(jnp.int32, (16, n), 0)
        hi = jnp.broadcast_to(hi.astype(F32), (16, n))
        lo = jnp.broadcast_to(lo.astype(F32), (16, n))
        weights2[...] = jnp.where(row == 0, hi, jnp.where(row == 1, lo, 0.0)).astype(BF16)
        acc[...] = jnp.zeros_like(acc)

    sums = lax.dot_general(x[...], weights2[...], NT, preferred_element_type=F32)
    col = 1.0 / (protos_all * jnp.sum(sums, axis=1, keepdims=True))
    col_out[...] = jnp.broadcast_to(col, (kb, 128)).T[:1, :]
    lanes = 512
    for r in range(0, n, lanes):
        v = x[:, r : r + lanes].astype(F32) * col
        acc[:, r : r + lanes] += jnp.sum(v.reshape(kb // 8, 8, lanes), axis=0)

    @pl.when(step == pl.num_programs(0) - 1)
    def _():
        part_out[...] = jnp.sum(acc[...], axis=0, keepdims=True) * factor[...]


def sweep(protos_all, x, weight, factor):
    width, n = x.shape
    kb = min(256, width)
    return pl.pallas_call(
        functools.partial(sweep_kernel, protos_all),
        grid=(width // kb,),
        in_specs=[pl.BlockSpec((kb, n), lambda i: (i, 0)), full((1, n)), full((1, n))],
        out_specs=[full((1, n)), pl.BlockSpec((1, kb), lambda i: (0, i))],
        out_shape=[
            jax.ShapeDtypeStruct((1, n), F32),
            jax.ShapeDtypeStruct((1, width), F32),
        ],
        scratch_shapes=[pltpu.VMEM((16, n), BF16), pltpu.VMEM((8, n), F32)],
        compiler_params=params(),
        cost_estimate=pl.CostEstimate(
            flops=4 * n * width, bytes_accessed=2 * n * width, transcendentals=0
        ),
        name="sweep",
    )(x, weight, factor)


def project_kernel(x, weight, student, out, weighted):
    n, depth = student.shape

    @pl.when(pl.program_id(0) == 0)
    def _():
        for r in range(0, n, 128):
            s = student[r : r + 128, :].astype(F32).T * weight[:, r : r + 128]
            hi, lo = split_hi_lo(s)
            weighted[:depth, r : r + 128] = hi
            weighted[depth:, r : r + 128] = lo

    g = lax.dot_general(x[...], weighted[...], NT, preferred_element_type=F32)
    out[...] = g[:, :depth] + g[:, depth:]


def project(x, weight, student):
    width, n = x.shape
    depth = student.shape[1]
    kb = min(256, width)
    return pl.pallas_call(
        project_kernel,
        grid=(width // kb,),
        in_specs=[pl.BlockSpec((kb, n), lambda i: (i, 0)), full((1, n)), full((n, depth))],
        out_specs=pl.BlockSpec((kb, depth), lambda i: (i, 0)),
        out_shape=jax.ShapeDtypeStruct((width, depth), F32),
        scratch_shapes=[pltpu.VMEM((2 * depth, n), BF16)],
        compiler_params=params(),
        cost_estimate=pl.CostEstimate(
            flops=2 * n * width * depth, bytes_accessed=2 * n * width, transcendentals=0
        ),
        name="project",
    )(x, weight, student)


def grad_kernel(scale, x, weight, student, first, col, out, weighted):
    n, depth = student.shape
    kb = x.shape[0]

    @pl.when(pl.program_id(0) == 0)
    def _():
        for r in range(0, n, 128):
            s = student[r : r + 128, :].astype(F32).T * weight[:, r : r + 128]
            hi, lo = split_hi_lo(s)
            weighted[:depth, r : r + 128] = hi
            weighted[depth:, r : r + 128] = lo

    g = lax.dot_general(x[...], weighted[...], NT, preferred_element_type=F32)
    g = g[:, :depth] + g[:, depth:]
    for k in range(0, kb, 128):
        a = first[k : k + 128, :].T
        b = g[k : k + 128, :].T
        out[:, k : k + 128] = (scale * (a - b * col[:, k : k + 128])).astype(BF16)


def proto_grad_columns(scale, x, weight, student, first, col):
    width, n = x.shape
    depth = student.shape[1]
    kb = min(256, width)
    return pl.pallas_call(
        functools.partial(grad_kernel, scale),
        grid=(width // kb,),
        in_specs=[
            pl.BlockSpec((kb, n), lambda i: (i, 0)),
            full((1, n)),
            full((n, depth)),
            pl.BlockSpec((kb, depth), lambda i: (i, 0)),
            pl.BlockSpec((1, kb), lambda i: (0, i)),
        ],
        out_specs=pl.BlockSpec((depth, kb), lambda i: (0, i)),
        out_shape=jax.ShapeDtypeStruct((depth, width), BF16),
        scratch_shapes=[pltpu.VMEM((2 * depth, n), BF16)],
        compiler_params=params(),
        cost_estimate=pl.CostEstimate(
            flops=2 * n * width * depth, bytes_accessed=2 * n * width, transcendentals=0
        ),
        name="proto_grad",
    )(x, weight, student, first, col)


def logit_kernel(protos_all, chunk, protos, crops, col, bias, grad_out, loss_out, bias_t, loss):
    step = pl.program_id(0)
    rows = grad_out.shape[0]
    width = protos.shape[1]

    @pl.when(step == 0)
    def _():
        bias_t[:rows, :] = jnp.broadcast_to(bias[0:1, :], (128, rows)).T
        bias_t[rows:, :] = jnp.broadcast_to(bias[1:2, :], (128, rows)).T
        loss[...] = jnp.zeros_like(loss)

    total = loss[...]
    for k in range(0, width, chunk):
        s = jnp.dot(crops[...], protos[:, k : k + chunk], preferred_element_type=F32)
        for j in range(0, chunk, 128):
            t = jnp.exp(s[:rows, j : j + 128] + bias_t[:rows, :]) * col[:, k + j : k + j + 128]
            log_probs = s[rows:, j : j + 128] + bias_t[rows:, :]
            g = protos_all * (jnp.exp(log_probs) - t)
            grad_out[:, k + j : k + j + 128] = g.astype(BF16)
            total = total + t * log_probs
    loss[...] = total

    @pl.when(step == pl.num_programs(0) - 1)
    def _():
        loss_out[...] = -jnp.sum(loss[...].T, axis=0, keepdims=True)


def logit_grads(protos_all, protos, crops, col, bias):
    depth, width = protos.shape
    rows = crops.shape[0] // 2
    cb = min(2048, width)
    return pl.pallas_call(
        functools.partial(logit_kernel, float(protos_all), min(256, cb)),
        grid=(width // cb,),
        in_specs=[
            pl.BlockSpec((depth, cb), lambda i: (0, i)),
            full((2 * rows, depth)),
            pl.BlockSpec((1, cb), lambda i: (0, i)),
            full((2, rows)),
        ],
        out_specs=[pl.BlockSpec((rows, cb), lambda i: (0, i)), full((1, rows))],
        out_shape=[
            jax.ShapeDtypeStruct((rows, width), BF16),
            jax.ShapeDtypeStruct((1, rows), F32),
        ],
        scratch_shapes=[pltpu.VMEM((2 * rows, 128), F32), pltpu.VMEM((rows, 128), F32)],
        compiler_params=params(),
        cost_estimate=pl.CostEstimate(
            flops=4 * rows * width * depth,
            bytes_accessed=2 * width * (rows + depth),
            transcendentals=2 * rows * width,
        ),
        name="logit_grads",
    )(protos, crops, col, bias)


def both(v):
    size = lax.axis_size("proto")
    if size == 2:
        return jnp.stack([v, lax.ppermute(v, "proto", [(0, 1), (1, 0)])])
    return lax.all_gather(v, "proto")


def from_all(v):
    size = lax.axis_size("dp")
    return lax.all_to_all(jnp.broadcast_to(v[None], (size,) + v.shape), "dp", 0, 0, tiled=True)


def merge(pairs):
    peak = jnp.max(pairs[:, 0], axis=0)
    total = jnp.sum(pairs[:, 1] * jnp.exp(pairs[:, 0] - peak), axis=0)
    return jnp.stack([peak, total])


def shards(teacher, student, prototypes):
    rows, depth = teacher.shape
    n = rows * lax.axis_size("dp")
    protos_all = prototypes.shape[1] * lax.axis_size("proto")
    gathered = lax.all_gather(prototypes, "dp", axis=0, tiled=True)
    own = lax.all_to_all(prototypes, "dp", 1, 0, tiled=True)
    teacher_all = from_all(teacher).reshape(n, depth)
    student_all = from_all(student).reshape(n, depth)

    x_t, peak_t, total_t = exp_rows(own, teacher_all)
    stats = from_all(merge(both(jnp.concatenate([peak_t, total_t]))))
    x_s, peak_s, total_s = exp_rows(own, student_all)
    stats = merge(stats)
    factor = jnp.exp(peak_t - stats[:1])
    weight = factor / stats[1:]
    glob_t = stats[:1]

    for it in range(ITERS):
        part, col = sweep(float(protos_all), x_t, weight, factor)
        if it == 0:
            st = merge(both(jnp.concatenate([peak_s, total_s])))
            got = from_all(jnp.concatenate([jnp.sum(both(part), axis=0), st]))
            total = jnp.sum(got[:, :1], axis=0)
            st = merge(got[:, 1:])
            glob_s, total_s = st[:1], st[1:]
            soft = project(x_s, jnp.exp(peak_s - glob_s) / total_s, student_all)
        elif it < ITERS - 1:
            total = jnp.sum(from_all(jnp.sum(both(part), axis=0)), axis=0)
        else:
            got = from_all(jnp.concatenate([jnp.sum(both(part), axis=0), col], axis=1))
            total = jnp.sum(got[:, :, :n], axis=0)
            col_all = got[:, 0, n:].reshape(1, -1)
        row_scale = 1.0 / (n * total)
        weight = row_scale * factor

    grad = proto_grad_columns(protos_all / 128.0, x_t, weight * n, student_all, soft, col)
    proto_grad = lax.all_to_all(grad, "dp", 0, 1, tiled=True)

    bias = jnp.concatenate([jnp.log(n * row_scale) - glob_t, -glob_s - jnp.log(total_s)])
    bias = lax.dynamic_slice_in_dim(bias, lax.axis_index("dp") * rows, rows, 1)
    logit_grad, loss = logit_grads(
        protos_all, gathered, jnp.concatenate([teacher, student]), col_all, bias
    )
    crop_loss = jnp.sum(both(loss[0]), axis=0)
    return crop_loss, logit_grad, proto_grad


def solution(mesh):
    placed = (P("dp", None), P("dp", None), P("dp", "proto"))
    return jax.shard_map(
        shards,
        mesh=mesh,
        in_specs=placed,
        out_specs=(P("dp"), P("dp", "proto"), P("dp", "proto")),
        check_vma=False,
    )
```

```python
import functools
import math

import jax
import jax.numpy as jnp
from jax import lax
from jax.experimental import pallas as pl
from jax.experimental.pallas import tpu as pltpu
from jax.sharding import PartitionSpec as P

ITERS = 3
F32 = jnp.float32
BF16 = jnp.bfloat16
NT = (((1,), (1,)), ((), ()))
EXTRA = 16
WHOLE = pl.BlockSpec(memory_space=pltpu.VMEM)


def params(mib):
    return pltpu.CompilerParams(vmem_limit_bytes=mib * 1024 * 1024)


def cost(flops, nbytes, exps=0):
    return pl.CostEstimate(flops=flops, bytes_accessed=nbytes, transcendentals=exps)


def full(shape):
    return pl.BlockSpec(shape, lambda i: (0,) * len(shape))


def pieces(v, count):
    out = []
    for _ in range(count):
        p = v.astype(BF16)
        out.append(p)
        v = v - p.astype(F32)
    return out


def rows_of(parts, height):
    n = parts[0].shape[1]
    row = lax.broadcasted_iota(jnp.int32, (height, n), 0)
    block = jnp.zeros((height, n), F32)
    for i, p in enumerate(parts):
        block = jnp.where(row == i, jnp.broadcast_to(p.astype(F32), (height, n)), block)
    return block.astype(BF16)


def exp_kernel(rb, kc, protos, crops, x, peak_out, lse_out, protos_t, scores_a, scores_b):
    width, n = x.shape
    blocks = n // rb
    for q in range(0, width, 128):
        protos_t[q : q + 128, :] = protos[:, q : q + 128].astype(F32).T.astype(BF16)

    def at(b):
        return pl.ds(pl.multiple_of(b * rb, rb), rb)

    def stage(new, new_scores, old, old_scores, peak):
        new_peak = jnp.full((8, rb), -jnp.inf, F32)
        total = jnp.zeros((8, rb), F32)
        for q in range(0, width, kc):
            if new is not None:
                s = lax.dot_general(
                    protos_t[q : q + kc, :], crops[at(new), :], NT, preferred_element_type=F32
                )
                new_scores[q : q + kc, :] = s
                new_peak = jnp.maximum(new_peak, jnp.max(s.reshape(kc // 8, 8, rb), axis=0))
            if old is not None:
                e = jnp.exp(old_scores[q : q + kc, :] - peak)
                total = total + jnp.sum(e.reshape(kc // 8, 8, rb), axis=0)
                x[q : q + kc, at(old)] = e.astype(BF16)
        if old is not None:
            peak_out[:, at(old)] = peak
            lse_out[:, at(old)] = peak + jnp.log(jnp.sum(total, axis=0, keepdims=True))
        return jnp.max(new_peak, axis=0, keepdims=True)

    def two(j, peak):
        peak = stage(2 * j + 1, scores_b, 2 * j, scores_a, peak)
        return stage(jnp.minimum(2 * j + 2, blocks - 1), scores_a, 2 * j + 1, scores_b, peak)

    lax.fori_loop(0, blocks // 2, two, stage(0, scores_a, None, None, None))


def exp_rows(protos, crops):
    depth, width = protos.shape
    n = crops.shape[0]
    rb = 512
    return pl.pallas_call(
        functools.partial(exp_kernel, rb, 128),
        in_specs=[WHOLE, WHOLE],
        out_specs=[WHOLE] * 3,
        out_shape=[
            jax.ShapeDtypeStruct((width, n), BF16),
            jax.ShapeDtypeStruct((1, n), F32),
            jax.ShapeDtypeStruct((1, n), F32),
        ],
        scratch_shapes=[
            pltpu.VMEM((width, depth), BF16),
            pltpu.VMEM((width, rb), F32),
            pltpu.VMEM((width, rb), F32),
        ],
        compiler_params=params(14),
        cost_estimate=cost(2 * n * width * depth, 2 * n * width, n * width),
        name="exp_rows",
    )(protos, crops)


def sweep_kernel(first, n_all, protos_all, count, x, lead, *refs):
    parts, (part_out, col_out, lead_out, weights, col_rows) = refs[:count], refs[count:]
    width, n = x.shape
    if first:
        peak = functools.reduce(
            jnp.maximum, [jnp.max(p[...], axis=0, keepdims=True) for p in parts]
        )
        total = sum(jnp.sum(jnp.exp(p[...] - peak), axis=0, keepdims=True) for p in parts)
        lse = peak + jnp.log(total)
        factor = jnp.exp(lead[...] - lse)
        weight = factor
        lead_out[0:1, :] = factor
        lead_out[1:2, :] = lse
    else:
        factor = lead[...]
        total = sum(jnp.sum(p[...], axis=0, keepdims=True) for p in parts)
        weight = factor / (n_all * total)
    weights[...] = rows_of(pieces(weight, 2), 16)
    sums = lax.dot_general(weights[...], x[...], NT, preferred_element_type=F32)
    col = 1.0 / (protos_all * jnp.sum(sums, axis=0, keepdims=True))
    col_out[...] = col
    col_rows[...] = rows_of(pieces(col, 2), 16)
    out = jnp.dot(col_rows[...], x[...], preferred_element_type=F32)
    part_out[...] = jnp.sum(out, axis=0, keepdims=True) * factor


def sweep(first, n_all, protos_all, x, lead, parts):
    width, n = x.shape
    return pl.pallas_call(
        functools.partial(sweep_kernel, first, float(n_all), float(protos_all), len(parts)),
        in_specs=[WHOLE] * (2 + len(parts)),
        out_specs=[WHOLE] * 3,
        out_shape=[
            jax.ShapeDtypeStruct((1, n), F32),
            jax.ShapeDtypeStruct((1, width), F32),
            jax.ShapeDtypeStruct((2, n), F32),
        ],
        scratch_shapes=[pltpu.VMEM((16, n), BF16), pltpu.VMEM((16, width), BF16)],
        compiler_params=params(8),
        cost_estimate=cost(4 * n * width, 2 * n * width),
        name="sweep",
    )(x, lead, *parts)


def weighted_student(weight, student, weighted):
    n, depth = student.shape
    for r in range(0, n, 128):
        s = student[r : r + 128, :].astype(F32).T * weight[:, r : r + 128]
        hi, lo = pieces(s, 2)
        weighted[:depth, r : r + 128] = hi
        weighted[depth:, r : r + 128] = lo


def soft_kernel(x, peak, lse, student, out, weighted):
    depth = student.shape[1]
    weighted_student(jnp.exp(peak[...] - lse[...]), student, weighted)
    g = lax.dot_general(x[...], weighted[...], NT, preferred_element_type=F32)
    out[...] = g[:, :depth] + g[:, depth:]


def soft_part(x, peak, lse, student):
    width, n = x.shape
    depth = student.shape[1]
    return pl.pallas_call(
        soft_kernel,
        in_specs=[WHOLE] * 4,
        out_specs=WHOLE,
        out_shape=jax.ShapeDtypeStruct((width, depth), F32),
        scratch_shapes=[pltpu.VMEM((2 * depth, n), BF16)],
        compiler_params=params(18),
        cost_estimate=cost(2 * n * width * depth, 2 * n * width),
        name="soft_part",
    )(x, peak, lse, student)


def grad_kernel(scale, x, weight, student, soft, col, out, weighted):
    width = x.shape[0]
    depth = student.shape[1]
    weighted_student(weight[...], student, weighted)
    g = lax.dot_general(x[...], weighted[...], NT, preferred_element_type=F32)
    g = g[:, :depth] + g[:, depth:]
    for k in range(0, width, 128):
        a = soft[k : k + 128, :].T
        b = g[k : k + 128, :].T
        out[:, k : k + 128] = (scale * (a - b * col[:, k : k + 128])).astype(BF16)


def proto_grad_columns(scale, x, weight, student, soft, col):
    width, n = x.shape
    depth = student.shape[1]
    return pl.pallas_call(
        functools.partial(grad_kernel, scale),
        in_specs=[WHOLE] * 5,
        out_specs=WHOLE,
        out_shape=jax.ShapeDtypeStruct((depth, width), BF16),
        scratch_shapes=[pltpu.VMEM((2 * depth, n), BF16)],
        compiler_params=params(18),
        cost_estimate=cost(2 * n * width * depth, 2 * n * width),
        name="proto_grad",
    )(x, weight, student, soft, col)


def logit_kernel(
    protos_all, chunk, protos, crops, col, bias, grad_out, loss_out, lhs, rhs, grads, loss, in_sem, out_sem
):
    slots, rows, cb = grads.shape
    depth, width = protos.shape
    steps = width // cb

    def fetch(c):
        at = pl.ds(c * cb, cb)
        return pltpu.make_async_copy(protos.at[:, at], rhs.at[:depth, at], in_sem.at[c])

    def store(c, slot):
        at = pl.ds(pl.multiple_of(c * cb, cb), cb)
        return pltpu.make_async_copy(grads.at[slot], grad_out.at[:, at], out_sem.at[slot])

    for c in range(steps):
        fetch(c).start()

    lhs[:, :depth] = crops[...]
    lane = lax.broadcasted_iota(jnp.int32, (rows, 128), 1)
    for i in range(2):
        b = jnp.broadcast_to(bias[i : i + 1, :], (128, rows)).T
        ext = jnp.zeros((rows, 128), F32)
        for j, p in enumerate(pieces(b, 3)):
            ext = jnp.where(lane == j, p.astype(F32), ext)
        if i == 0:
            ext = jnp.where((lane >= 3) & (lane < 6), 1.0, ext)
        lhs[i * rows : (i + 1) * rows, depth:] = ext.astype(BF16)[:, :EXTRA]
    one = jnp.ones((1, cb), F32)
    for c in range(steps):
        at = slice(c * cb, (c + 1) * cb)
        log_col = jnp.log(protos_all * col[:, at])
        rhs[depth:, at] = rows_of([one] * 3 + pieces(log_col, 3), EXTRA)
    loss[...] = jnp.zeros_like(loss)

    @pl.loop(0, steps)
    def _(c):
        slot = lax.rem(c, slots)

        @pl.when(c >= slots)
        def _():
            store(c - slots, slot).wait()

        pltpu.make_async_copy(
            protos.at[:, pl.ds(0, cb)], rhs.at[:depth, pl.ds(0, cb)], in_sem.at[c]
        ).wait()
        total = loss[...]
        for k in range(0, cb, chunk):
            at = pl.ds(pl.multiple_of(c * cb + k, chunk), chunk)
            s = jnp.dot(lhs[...], rhs[:, at], preferred_element_type=F32)
            for j in range(0, chunk, 128):
                t = jnp.exp(s[:rows, j : j + 128])
                u = s[rows:, j : j + 128]
                grads[slot, :, k + j : k + j + 128] = (jnp.exp(u) - t).astype(BF16)
                total = total + t * u
        loss[...] = total
        store(c, slot).start()

    for c in range(max(0, steps - slots), steps):
        store(c, c % slots).wait()
    loss_out[...] = jnp.sum(loss[...].T, axis=0, keepdims=True)


def logit_grads(protos_all, protos, crops, col, bias):
    depth, width = protos.shape
    rows = crops.shape[0] // 2
    cb = min(2048, width)
    slots = min(4, width // cb)
    return pl.pallas_call(
        functools.partial(logit_kernel, float(protos_all), min(256, cb)),
        in_specs=[pl.BlockSpec(memory_space=pltpu.HBM), WHOLE, WHOLE, WHOLE],
        out_specs=[pl.BlockSpec(memory_space=pltpu.HBM), WHOLE],
        out_shape=[
            jax.ShapeDtypeStruct((rows, width), BF16),
            jax.ShapeDtypeStruct((1, rows), F32),
        ],
        scratch_shapes=[
            pltpu.VMEM((2 * rows, depth + EXTRA), BF16),
            pltpu.VMEM((depth + EXTRA, width), BF16),
            pltpu.VMEM((slots, rows, cb), BF16),
            pltpu.VMEM((rows, 128), F32),
            pltpu.SemaphoreType.DMA((width // cb,)),
            pltpu.SemaphoreType.DMA((slots,)),
        ],
        compiler_params=params(22),
        cost_estimate=cost(
            4 * rows * width * depth, 2 * width * (rows + depth), 2 * rows * width
        ),
        name="logit_grads",
    )(protos, crops, col, bias)


def over_proto(v, combine):
    size = lax.axis_size("proto")
    if size == 2:
        return combine([v, lax.ppermute(v, "proto", [(0, 1), (1, 0)])])
    got = lax.all_gather(v, "proto")
    return combine([got[i] for i in range(size)])


def add(parts):
    return functools.reduce(jnp.add, parts)


def log_add(parts):
    peak = functools.reduce(jnp.maximum, parts)
    return peak + jnp.log(sum(jnp.exp(p - peak) for p in parts))


def dp_rounds():
    size = lax.axis_size("dp")
    rounds, bit = [], 1
    while bit < size:
        step = min(4, size // bit)
        rounds.append([s * bit for s in range(1, step)])
        bit *= step
    return rounds[::-1]


def swap(v, mask):
    size = lax.axis_size("dp")
    return lax.ppermute(v, "dp", [(a, a ^ mask) for a in range(size)])


def from_partners(v, masks):
    return [v] + [swap(v, m) for m in masks]


def radix4(v, combine):
    rounds = dp_rounds()
    for i, masks in enumerate(rounds):
        got = from_partners(v, masks)
        if i == len(rounds) - 1:
            return got
        v = combine(got)


def in_dp_order(v):
    rest = v.shape[1:]
    size = lax.axis_size("dp")
    me = lax.axis_index("dp")
    bit = 1
    while bit < size:
        w = v.reshape((size // (2 * bit), 2, bit) + rest)
        w = jnp.where((me & bit) != 0, w[:, ::-1], w)
        v = w.reshape((size,) + rest)
        bit *= 2
    return v


def gather_round(v, masks):
    return jnp.stack(from_partners(v, masks), axis=1).reshape((-1,) + v.shape[1:])


def own_share(v):
    size = lax.axis_size("proto")
    rows = v.shape[0] // size
    return lax.dynamic_slice_in_dim(v, lax.axis_index("proto") * rows, rows, 0)


def both_shares(v):
    size = lax.axis_size("proto")
    if size == 2:
        other = lax.ppermute(v, "proto", [(0, 1), (1, 0)])
        mine = lax.axis_index("proto") == 0
        return jnp.concatenate([jnp.where(mine, v, other), jnp.where(mine, other, v)], axis=1)
    return lax.all_gather(v, "proto", axis=1, tiled=True)


def shards(teacher, student, prototypes):
    rows, depth = teacher.shape
    dp = lax.axis_size("dp")
    n = rows * dp
    protos_all = prototypes.shape[1] * lax.axis_size("proto")
    width = prototypes.shape[1] // dp

    own = lax.all_to_all(prototypes, "dp", 1, 0, tiled=True)
    crops = jnp.stack([own_share(teacher), own_share(student)])[None]
    rounds = dp_rounds()
    for masks in rounds[:-1]:
        crops = gather_round(crops, masks)
    own, crops, prototypes = lax.optimization_barrier((own, crops, prototypes))
    gathered = lax.all_gather(prototypes, "dp", axis=0, tiled=True)
    teacher_all, student_all = [
        both_shares(in_dp_order(gather_round(crops[:, i], rounds[-1]))).reshape(n, depth)
        for i in range(2)
    ]

    x_t, peak_t, lse_t = exp_rows(own, teacher_all)
    x_s, peak_s, lse_s = exp_rows(own, student_all)
    lses = radix4(over_proto(jnp.concatenate([lse_t, lse_s]), log_add), log_add)
    glob_s = log_add([p[1:] for p in lses])
    soft = soft_part(x_s, peak_s, glob_s, student_all)

    part, col, lead = sweep(True, n, protos_all, x_t, peak_t, [p[:1] for p in lses])
    factor, glob_t = lead[:1], lead[1:]
    for it in range(1, ITERS):
        part, col, _ = sweep(
            False, n, protos_all, x_t, factor, radix4(over_proto(part, add), add)
        )

    total, cols = over_proto(part, add), col[None]
    for masks in dp_rounds():
        got = from_partners(jnp.concatenate([total, cols.reshape(1, -1)], axis=1), masks)
        total = add([g[:, :n] for g in got])
        cols = jnp.stack([g[:, n:].reshape(cols.shape) for g in got], axis=1)
        cols = cols.reshape(-1, 1, width)
    row_scale = 1.0 / (n * total)
    col_all = in_dp_order(cols).reshape(1, -1)

    grad = proto_grad_columns(
        protos_all / 128.0, x_t, n * row_scale * factor, student_all, soft, col
    )
    proto_grad = lax.all_to_all(grad, "dp", 0, 1, tiled=True)

    log_protos = math.log(protos_all)
    bias = jnp.concatenate([jnp.log(n * row_scale) - glob_t, log_protos - glob_s])
    bias = lax.dynamic_slice_in_dim(bias, lax.axis_index("dp") * rows, rows, 1)
    logit_grad, loss = logit_grads(
        protos_all, gathered, jnp.concatenate([teacher, student]), col_all, bias
    )
    crop_loss = log_protos - over_proto(loss[0], add) / protos_all
    return crop_loss, logit_grad, proto_grad


def solution(mesh):
    placed = (P("dp", None), P("dp", None), P("dp", "proto"))
    return jax.shard_map(
        shards,
        mesh=mesh,
        in_specs=placed,
        out_specs=(P("dp"), P("dp", "proto"), P("dp", "proto")),
        check_vma=False,
    )
```

```python
import functools
import math

import jax
import jax.numpy as jnp
from jax import lax
from jax.experimental import pallas as pl
from jax.experimental.pallas import tpu as pltpu
from jax.sharding import PartitionSpec as P

ITERS = 3
F32 = jnp.float32
BF16 = jnp.bfloat16
NT = (((1,), (1,)), ((), ()))
EXTRA = 16
WHOLE = pl.BlockSpec(memory_space=pltpu.VMEM)
FAR = pl.BlockSpec(memory_space=pltpu.HBM)


def params(mib):
    return pltpu.CompilerParams(vmem_limit_bytes=mib * 1024 * 1024)


def cost(flops, nbytes, exps=0):
    return pl.CostEstimate(flops=flops, bytes_accessed=nbytes, transcendentals=exps)


def near(x):
    return pltpu.with_memory_space_constraint(x, pltpu.VMEM)


def far(x):
    return pltpu.with_memory_space_constraint(x, pltpu.HBM)


def full(shape):
    return pl.BlockSpec(shape, lambda i: (0,) * len(shape))


def pieces(v, count):
    out = []
    for _ in range(count):
        p = v.astype(BF16)
        out.append(p)
        v = v - p.astype(F32)
    return out


def rows_of(parts, height):
    n = parts[0].shape[1]
    row = lax.broadcasted_iota(jnp.int32, (height, n), 0)
    block = jnp.zeros((height, n), F32)
    for i, p in enumerate(parts):
        block = jnp.where(row == i, jnp.broadcast_to(p.astype(F32), (height, n)), block)
    return block.astype(BF16)


def exp_kernel(
    rb, kc, resident, protos, crops, x, peak_out, lse_out, protos_t, scores_a, scores_b, *refs
):
    width, n = x.shape
    blocks = n // rb
    for q in range(0, width, 128):
        protos_t[q : q + 128, :] = protos[:, q : q + 128].astype(F32).T.astype(BF16)

    def at(b):
        return pl.ds(pl.multiple_of(b * rb, rb), rb)

    def leave(b, slot):
        return pltpu.make_async_copy(refs[0].at[slot], x.at[:, at(b)], refs[1].at[slot])

    def stage(new, new_scores, old, old_scores, peak, slot=0):
        new_peak = jnp.full((8, rb), -jnp.inf, F32)
        total = jnp.zeros((8, rb), F32)
        for q in range(0, width, kc):
            if new is not None:
                s = lax.dot_general(
                    protos_t[q : q + kc, :], crops[at(new), :], NT, preferred_element_type=F32
                )
                new_scores[q : q + kc, :] = s
                new_peak = jnp.maximum(new_peak, jnp.max(s.reshape(kc // 8, 8, rb), axis=0))
            if old is not None:
                e = jnp.exp(old_scores[q : q + kc, :] - peak)
                total = total + jnp.sum(e.reshape(kc // 8, 8, rb), axis=0)
                if resident:
                    x[q : q + kc, at(old)] = e.astype(BF16)
                else:
                    refs[0][slot, q : q + kc, :] = e.astype(BF16)
        if old is not None:
            peak_out[:, at(old)] = peak
            lse_out[:, at(old)] = peak + jnp.log(jnp.sum(total, axis=0, keepdims=True))
            if not resident:
                leave(old, slot).start()
        return jnp.max(new_peak, axis=0, keepdims=True)

    def free(j, slot):
        if not resident:

            @pl.when(j > 0)
            def _():
                leave(2 * j - 2 + slot, slot).wait()

    def two(j, peak):
        free(j, 0)
        peak = stage(2 * j + 1, scores_b, 2 * j, scores_a, peak, 0)
        free(j, 1)
        return stage(jnp.minimum(2 * j + 2, blocks - 1), scores_a, 2 * j + 1, scores_b, peak, 1)

    lax.fori_loop(0, blocks // 2, two, stage(0, scores_a, None, None, None))
    if not resident:
        leave(blocks - 2, 0).wait()
        leave(blocks - 1, 1).wait()


def exp_rows(protos, crops, resident):
    depth, width = protos.shape
    n = crops.shape[0]
    rb = 512
    leaving = [pltpu.VMEM((2, width, rb), BF16), pltpu.SemaphoreType.DMA((2,))]
    return pl.pallas_call(
        functools.partial(exp_kernel, rb, 128, resident),
        in_specs=[WHOLE, WHOLE],
        out_specs=[WHOLE if resident else FAR, WHOLE, WHOLE],
        out_shape=[
            (pltpu.VMEM if resident else pltpu.HBM)((width, n), BF16),
            jax.ShapeDtypeStruct((1, n), F32),
            jax.ShapeDtypeStruct((1, n), F32),
        ],
        scratch_shapes=[
            pltpu.VMEM((width, depth), BF16),
            pltpu.VMEM((width, rb), F32),
            pltpu.VMEM((width, rb), F32),
        ]
        + ([] if resident else leaving),
        compiler_params=params(14 if resident else 18),
        cost_estimate=cost(2 * n * width * depth, 2 * n * width, n * width),
        name="exp_rows",
    )(protos, crops)


def sweep_kernel(first, n_all, protos_all, count, x, lead, *refs):
    parts, (part_out, col_out, lead_out, weights, col_rows) = refs[:count], refs[count:]
    width, n = x.shape
    if first:
        peak = functools.reduce(
            jnp.maximum, [jnp.max(p[...], axis=0, keepdims=True) for p in parts]
        )
        total = sum(jnp.sum(jnp.exp(p[...] - peak), axis=0, keepdims=True) for p in parts)
        lse = peak + jnp.log(total)
        factor = jnp.exp(lead[...] - lse)
        weight = factor
        lead_out[0:1, :] = factor
        lead_out[1:2, :] = lse
    else:
        factor = lead[...]
        total = sum(jnp.sum(p[...], axis=0, keepdims=True) for p in parts)
        weight = factor / (n_all * total)
    weights[...] = rows_of(pieces(weight, 2), 16)
    sums = lax.dot_general(weights[...], x[...], NT, preferred_element_type=F32)
    col = 1.0 / (protos_all * jnp.sum(sums, axis=0, keepdims=True))
    col_out[...] = col
    col_rows[...] = rows_of(pieces(col, 2), 16)
    out = jnp.dot(col_rows[...], x[...], preferred_element_type=F32)
    part_out[...] = jnp.sum(out, axis=0, keepdims=True) * factor


def sweep(first, n_all, protos_all, x, lead, parts):
    width, n = x.shape
    return pl.pallas_call(
        functools.partial(sweep_kernel, first, float(n_all), float(protos_all), len(parts)),
        in_specs=[WHOLE] * (2 + len(parts)),
        out_specs=[WHOLE] * 3,
        out_shape=[
            jax.ShapeDtypeStruct((1, n), F32),
            jax.ShapeDtypeStruct((1, width), F32),
            jax.ShapeDtypeStruct((2, n), F32),
        ],
        scratch_shapes=[pltpu.VMEM((16, n), BF16), pltpu.VMEM((16, width), BF16)],
        compiler_params=params(8),
        cost_estimate=cost(4 * n * width, 2 * n * width),
        name="sweep",
    )(near(x), lead, *parts)


def weighted_student(weight, student, weighted):
    n, depth = student.shape
    for r in range(0, n, 128):
        s = student[r : r + 128, :].astype(F32).T * weight[:, r : r + 128]
        hi, lo = pieces(s, 2)
        weighted[:depth, r : r + 128] = hi
        weighted[depth:, r : r + 128] = lo


def soft_kernel(x, peak, lse, student, out, weighted):
    depth = student.shape[1]

    @pl.when(pl.program_id(0) == 0)
    def _():
        weighted_student(jnp.exp(peak[...] - lse[...]), student, weighted)

    g = lax.dot_general(x[...], weighted[...], NT, preferred_element_type=F32)
    out[...] = g[:, :depth] + g[:, depth:]


def soft_part(x, peak, lse, student):
    width, n = x.shape
    depth = student.shape[1]
    kb = min(512, width)
    return pl.pallas_call(
        soft_kernel,
        grid=(width // kb,),
        in_specs=[
            pl.BlockSpec((kb, n), lambda i: (i, 0)),
            full((1, n)),
            full((1, n)),
            full((n, depth)),
        ],
        out_specs=pl.BlockSpec((kb, depth), lambda i: (i, 0)),
        out_shape=jax.ShapeDtypeStruct((width, depth), F32),
        scratch_shapes=[pltpu.VMEM((2 * depth, n), BF16)],
        compiler_params=params(24),
        cost_estimate=cost(2 * n * width * depth, 2 * n * width),
        name="soft_part",
    )(far(x), peak, lse, student)


def grad_kernel(scale, x, weight, student, soft, col, out, weighted):
    width = x.shape[0]
    depth = student.shape[1]
    weighted_student(weight[...], student, weighted)
    g = lax.dot_general(x[...], weighted[...], NT, preferred_element_type=F32)
    g = g[:, :depth] + g[:, depth:]
    for k in range(0, width, 128):
        a = soft[k : k + 128, :].T
        b = g[k : k + 128, :].T
        out[:, k : k + 128] = (scale * (a - b * col[:, k : k + 128])).astype(BF16)


def proto_grad_columns(scale, x, weight, student, soft, col):
    width, n = x.shape
    depth = student.shape[1]
    return pl.pallas_call(
        functools.partial(grad_kernel, scale),
        in_specs=[WHOLE] * 5,
        out_specs=WHOLE,
        out_shape=jax.ShapeDtypeStruct((depth, width), BF16),
        scratch_shapes=[pltpu.VMEM((2 * depth, n), BF16)],
        compiler_params=params(18),
        cost_estimate=cost(2 * n * width * depth, 2 * n * width),
        name="proto_grad",
    )(near(x), weight, student, soft, col)


def logit_kernel(
    protos_all, chunk, protos, crops, col, bias, grad_out, loss_out, lhs, rhs, grads, loss, in_sem, out_sem
):
    slots, rows, cb = grads.shape
    depth, width = protos.shape
    steps = width // cb

    def fetch(c):
        at = pl.ds(c * cb, cb)
        return pltpu.make_async_copy(protos.at[:, at], rhs.at[:depth, at], in_sem.at[c])

    def store(c, slot):
        at = pl.ds(pl.multiple_of(c * cb, cb), cb)
        return pltpu.make_async_copy(grads.at[slot], grad_out.at[:, at], out_sem.at[slot])

    for c in range(steps):
        fetch(c).start()

    lhs[:, :depth] = crops[...]
    first = pl.multiple_of(lax.axis_index("dp") * rows, rows)
    lane = lax.broadcasted_iota(jnp.int32, (rows, 128), 1)
    for i in range(2):
        b = jnp.broadcast_to(bias[i : i + 1, pl.ds(first, rows)], (128, rows)).T
        ext = jnp.zeros((rows, 128), F32)
        for j, p in enumerate(pieces(b, 3)):
            ext = jnp.where(lane == j, p.astype(F32), ext)
        if i == 0:
            ext = jnp.where((lane >= 3) & (lane < 6), 1.0, ext)
        lhs[i * rows : (i + 1) * rows, depth:] = ext.astype(BF16)[:, :EXTRA]
    one = jnp.ones((1, cb), F32)
    for c in range(steps):
        at = slice(c * cb, (c + 1) * cb)
        log_col = jnp.log(protos_all * col[:, at])
        rhs[depth:, at] = rows_of([one] * 3 + pieces(log_col, 3), EXTRA)
    loss[...] = jnp.zeros_like(loss)

    @pl.loop(0, steps)
    def _(c):
        slot = lax.rem(c, slots)

        @pl.when(c >= slots)
        def _():
            store(c - slots, slot).wait()

        pltpu.make_async_copy(
            protos.at[:, pl.ds(0, cb)], rhs.at[:depth, pl.ds(0, cb)], in_sem.at[c]
        ).wait()
        half = rows // 2
        for k in range(0, cb, chunk):
            at = pl.ds(pl.multiple_of(c * cb + k, chunk), chunk)
            for r in (0, half):
                here = slice(r, r + half)
                t = jnp.exp(jnp.dot(lhs[here, :], rhs[:, at], preferred_element_type=F32))
                u = jnp.dot(
                    lhs[rows + r : rows + r + half, :], rhs[:, at], preferred_element_type=F32
                )
                grads[slot, here, k : k + chunk] = (jnp.exp(u) - t).astype(BF16)
                p = t * u
                loss[here, :] += sum(p[:, j : j + 128] for j in range(0, chunk, 128))
        store(c, slot).start()

    for c in range(max(0, steps - slots), steps):
        store(c, c % slots).wait()
    loss_out[...] = jnp.sum(loss[...].T, axis=0, keepdims=True)


def logit_grads(protos_all, protos, crops, col, bias):
    depth, width = protos.shape
    rows = crops.shape[0] // 2
    cb = min(4096, width)
    slots = min(4, width // cb)
    return pl.pallas_call(
        functools.partial(logit_kernel, float(protos_all), min(256, cb)),
        in_specs=[FAR, WHOLE, WHOLE, WHOLE],
        out_specs=[FAR, WHOLE],
        out_shape=[
            pltpu.HBM((rows, width), BF16),
            jax.ShapeDtypeStruct((1, rows), F32),
        ],
        scratch_shapes=[
            pltpu.VMEM((2 * rows, depth + EXTRA), BF16),
            pltpu.VMEM((depth + EXTRA, width), BF16),
            pltpu.VMEM((slots, rows, cb), BF16),
            pltpu.VMEM((rows, 128), F32),
            pltpu.SemaphoreType.DMA((width // cb,)),
            pltpu.SemaphoreType.DMA((slots,)),
        ],
        compiler_params=params(58),
        cost_estimate=cost(
            4 * rows * width * depth, 2 * width * (rows + depth), 2 * rows * width
        ),
        name="logit_grads",
    )(far(protos), crops, col, bias)


def over_proto(v, combine):
    size = lax.axis_size("proto")
    if size == 2:
        return combine([v, lax.ppermute(v, "proto", [(0, 1), (1, 0)])])
    got = lax.all_gather(v, "proto")
    return combine([got[i] for i in range(size)])


def add(parts):
    return functools.reduce(jnp.add, parts)


def log_add(parts):
    peak = functools.reduce(jnp.maximum, parts)
    return peak + jnp.log(sum(jnp.exp(p - peak) for p in parts))


def dp_rounds():
    size = lax.axis_size("dp")
    rounds, bit = [], 1
    while bit < size:
        step = min(4, size // bit)
        rounds.append([s * bit for s in range(1, step)])
        bit *= step
    return rounds[::-1]


def swap(v, mask):
    size = lax.axis_size("dp")
    return lax.ppermute(v, "dp", [(a, a ^ mask) for a in range(size)])


def from_partners(v, masks):
    return [v] + [swap(v, m) for m in masks]


def radix4(v, combine, fill=None):
    rounds = dp_rounds()
    out = None
    for i, masks in enumerate(rounds):
        got = from_partners(v, masks)
        if i == 0 and fill is not None:
            out = fill()
            got, out = lax.optimization_barrier((got, out))
        if i == len(rounds) - 1:
            return got, out
        v = combine(got)


def in_dp_order(v):
    rest = v.shape[1:]
    size = lax.axis_size("dp")
    me = lax.axis_index("dp")
    bit = 1
    while bit < size:
        w = v.reshape((size // (2 * bit), 2, bit) + rest)
        w = jnp.where((me & bit) != 0, w[:, ::-1], w)
        v = w.reshape((size,) + rest)
        bit *= 2
    return v


def gather_round(v, masks):
    return jnp.stack(from_partners(v, masks), axis=1).reshape((-1,) + v.shape[1:])


def own_share(v):
    size = lax.axis_size("proto")
    rows = v.shape[0] // size
    return lax.dynamic_slice_in_dim(v, lax.axis_index("proto") * rows, rows, 0)


def both_shares(v):
    size = lax.axis_size("proto")
    if size == 2:
        other = lax.ppermute(v, "proto", [(0, 1), (1, 0)])
        mine = lax.axis_index("proto") == 0
        return jnp.concatenate([jnp.where(mine, v, other), jnp.where(mine, other, v)], axis=1)
    return lax.all_gather(v, "proto", axis=1, tiled=True)


def shards(teacher, student, prototypes):
    rows, depth = teacher.shape
    dp = lax.axis_size("dp")
    n = rows * dp
    protos_all = prototypes.shape[1] * lax.axis_size("proto")
    width = prototypes.shape[1] // dp

    own = lax.all_to_all(prototypes, "dp", 1, 0, tiled=True)
    crops = jnp.stack([own_share(teacher), own_share(student)])[None]
    rounds = dp_rounds()
    for masks in rounds[:-1]:
        crops = gather_round(crops, masks)
    own, crops, prototypes = lax.optimization_barrier((own, crops, prototypes))
    gathered = lax.all_gather(prototypes, "dp", axis=0, tiled=True)
    teacher_all, student_all = [
        both_shares(in_dp_order(gather_round(crops[:, i], rounds[-1]))).reshape(n, depth)
        for i in range(2)
    ]

    x_t, peak_t, lse_t = exp_rows(own, teacher_all, True)
    lses, (x_s, peak_s, lse_s) = radix4(
        over_proto(lse_t, log_add), log_add, lambda: exp_rows(own, student_all, False)
    )
    part, col, lead = sweep(True, n, protos_all, x_t, peak_t, lses)
    factor, glob_t = lead[:1], lead[1:]

    def mixed(parts):
        return jnp.concatenate([add([p[:1] for p in parts]), log_add([p[1:] for p in parts])])

    soft = None
    for it in range(1, ITERS):
        part = over_proto(part, add)
        if it == 1:
            got, _ = radix4(jnp.concatenate([part, over_proto(lse_s, log_add)]), mixed)
            glob_s = log_add([p[1:] for p in got])
            got = [p[:1] for p in got]
        else:
            got, soft = radix4(part, add, lambda: soft_part(x_s, peak_s, glob_s, student_all))
        part, col, _ = sweep(False, n, protos_all, x_t, factor, got)

    total, cols = over_proto(part, add), col[None]
    for masks in dp_rounds():
        got = from_partners(jnp.concatenate([total, cols.reshape(1, -1)], axis=1), masks)
        total = add([g[:, :n] for g in got])
        cols = jnp.stack([g[:, n:].reshape(cols.shape) for g in got], axis=1)
        cols = cols.reshape(-1, 1, width)
    row_scale = 1.0 / (n * total)
    col_all = in_dp_order(cols).reshape(1, -1)

    grad = proto_grad_columns(
        protos_all / 128.0, x_t, n * row_scale * factor, student_all, soft, col
    )
    proto_grad = lax.all_to_all(grad, "dp", 0, 1, tiled=True)

    log_protos = math.log(protos_all)
    bias = jnp.concatenate([jnp.log(n * row_scale) - glob_t, log_protos - glob_s])
    logit_grad, loss = logit_grads(
        protos_all, gathered, jnp.concatenate([teacher, student]), col_all, bias
    )
    crop_loss = log_protos - over_proto(loss[0], add) / protos_all
    return crop_loss, logit_grad, proto_grad


def solution(mesh):
    placed = (P("dp", None), P("dp", None), P("dp", "proto"))
    return jax.shard_map(
        shards,
        mesh=mesh,
        in_specs=placed,
        out_specs=(P("dp"), P("dp", "proto"), P("dp", "proto")),
        check_vma=False,
    )
```

```python
import functools
import math

import jax
import jax.numpy as jnp
from jax import lax
from jax.experimental import pallas as pl
from jax.experimental.pallas import tpu as pltpu
from jax.sharding import PartitionSpec as P

ITERS = 3
F32 = jnp.float32
BF16 = jnp.bfloat16
NT = (((1,), (1,)), ((), ()))
EXTRA = 16
WHOLE = pl.BlockSpec(memory_space=pltpu.VMEM)
FAR = pl.BlockSpec(memory_space=pltpu.HBM)


def params(mib):
    return pltpu.CompilerParams(vmem_limit_bytes=mib * 1024 * 1024)


def cost(flops, nbytes, exps=0):
    return pl.CostEstimate(flops=flops, bytes_accessed=nbytes, transcendentals=exps)


def near(x):
    return pltpu.with_memory_space_constraint(x, pltpu.VMEM)


def far(x):
    return pltpu.with_memory_space_constraint(x, pltpu.HBM)


def full(shape):
    return pl.BlockSpec(shape, lambda i: (0,) * len(shape))


def pieces(v, count):
    out = []
    for _ in range(count):
        p = v.astype(BF16)
        out.append(p)
        v = v - p.astype(F32)
    return out


def rows_of(parts, height):
    n = parts[0].shape[1]
    row = lax.broadcasted_iota(jnp.int32, (height, n), 0)
    block = jnp.zeros((height, n), F32)
    for i, p in enumerate(parts):
        block = jnp.where(row == i, jnp.broadcast_to(p.astype(F32), (height, n)), block)
    return block.astype(BF16)


def exp_kernel(
    rb, kc, resident, protos, crops, x, peak_out, lse_out, protos_t, scores_a, scores_b, *refs
):
    width, n = x.shape
    blocks = n // rb
    for q in range(0, width, 128):
        protos_t[q : q + 128, :] = protos[:, q : q + 128].astype(F32).T.astype(BF16)

    def at(b):
        return pl.ds(b * rb if isinstance(b, int) else pl.multiple_of(b * rb, rb), rb)

    def leave(b, slot):
        return pltpu.make_async_copy(refs[0].at[slot], x.at[:, at(b)], refs[1].at[slot])

    def stage(new, new_scores, old, old_scores, peak, slot=0):
        new_peak = jnp.full((8, rb), -jnp.inf, F32)
        total = jnp.zeros((8, rb), F32)
        for q in range(0, width, kc):
            if new is not None:
                s = lax.dot_general(
                    protos_t[q : q + kc, :], crops[at(new), :], NT, preferred_element_type=F32
                )
                new_scores[q : q + kc, :] = s
                new_peak = jnp.maximum(new_peak, jnp.max(s.reshape(kc // 8, 8, rb), axis=0))
            if old is not None:
                e = jnp.exp(old_scores[q : q + kc, :] - peak)
                total = total + jnp.sum(e.reshape(kc // 8, 8, rb), axis=0)
                if resident:
                    x[q : q + kc, at(old)] = e.astype(BF16)
                else:
                    refs[0][slot, q : q + kc, :] = e.astype(BF16)
        if old is not None:
            peak_out[:, at(old)] = peak
            lse_out[:, at(old)] = peak + jnp.log(jnp.sum(total, axis=0, keepdims=True))
            if not resident:
                leave(old, slot).start()
        return jnp.max(new_peak, axis=0, keepdims=True)

    def free(j, slot):
        if not resident and not (isinstance(j, int) and j == 0):

            @pl.when(j > 0)
            def _():
                leave(2 * j - 2 + slot, slot).wait()

    def two(j, peak):
        free(j, 0)
        peak = stage(2 * j + 1, scores_b, 2 * j, scores_a, peak, 0)
        free(j, 1)
        return stage(2 * j + 2, scores_a, 2 * j + 1, scores_b, peak, 1)

    last = blocks // 2 - 1
    peak = lax.fori_loop(0, last, two, stage(0, scores_a, None, None, None))
    free(last, 0)
    peak = stage(blocks - 1, scores_b, blocks - 2, scores_a, peak, 0)
    free(last, 1)
    stage(None, None, blocks - 1, scores_b, peak, 1)
    if not resident:
        leave(blocks - 2, 0).wait()
        leave(blocks - 1, 1).wait()


def exp_rows(protos, crops, resident):
    depth, width = protos.shape
    n = crops.shape[0]
    rb = 512
    leaving = [pltpu.VMEM((2, width, rb), BF16), pltpu.SemaphoreType.DMA((2,))]
    return pl.pallas_call(
        functools.partial(exp_kernel, rb, 128, resident),
        in_specs=[WHOLE, WHOLE],
        out_specs=[WHOLE if resident else FAR, WHOLE, WHOLE],
        out_shape=[
            (pltpu.VMEM if resident else pltpu.HBM)((width, n), BF16),
            jax.ShapeDtypeStruct((1, n), F32),
            jax.ShapeDtypeStruct((1, n), F32),
        ],
        scratch_shapes=[
            pltpu.VMEM((width, depth), BF16),
            pltpu.VMEM((width, rb), F32),
            pltpu.VMEM((width, rb), F32),
        ]
        + ([] if resident else leaving),
        compiler_params=params(18 if resident else 22),
        cost_estimate=cost(2 * n * width * depth, 2 * n * width, n * width),
        name="exp_rows",
    )(protos, crops)


def sweep_kernel(first, n_all, protos_all, count, x, lead, *refs):
    parts, (part_out, col_out, lead_out, weights, acc) = refs[:count], refs[count:]
    width, n = x.shape
    if first:
        peak = functools.reduce(
            jnp.maximum, [jnp.max(p[...], axis=0, keepdims=True) for p in parts]
        )
        total = sum(jnp.sum(jnp.exp(p[...] - peak), axis=0, keepdims=True) for p in parts)
        lse = peak + jnp.log(total)
        factor = jnp.exp(lead[...] - lse)
        weight = factor
        lead_out[0:1, :] = factor
        lead_out[1:2, :] = lse
    else:
        factor = lead[...]
        total = sum(jnp.sum(p[...], axis=0, keepdims=True) for p in parts)
        weight = factor / (n_all * total)
    weights[...] = jnp.broadcast_to(weight, weights.shape)
    acc[...] = jnp.zeros_like(acc)
    kb = min(512, width)
    row = lax.broadcasted_iota(jnp.int32, (16, kb), 0)

    def scales(q):
        sums = jnp.zeros((kb // 8, 8, 128), F32)
        for r in range(0, n, 128):
            v = x[pl.ds(q, kb), r : r + 128].astype(F32)
            sums = sums + v.reshape(kb // 8, 8, 128) * weights[:, r : r + 128][None]
        sums = sums.reshape(kb, 128)
        sums = [jnp.sum(sums[i : i + 128].T, axis=0, keepdims=True) for i in range(0, kb, 128)]
        return 1.0 / (protos_all * jnp.concatenate(sums, axis=1))

    def totals(q, col):
        col_out[:, pl.ds(q, kb)] = col
        hi = col.astype(BF16).astype(F32)
        rows = jnp.where(row == 0, hi, jnp.where(row == 1, col - hi, 0.0)).astype(BF16)
        acc[...] += jnp.dot(rows, x[pl.ds(q, kb), :], preferred_element_type=F32)

    def both(i, col):
        q = pl.multiple_of(i * kb, kb)
        later = scales(pl.multiple_of(q + kb, kb))
        totals(q, col)
        return later

    totals(width - kb, lax.fori_loop(0, width // kb - 1, both, scales(0)))
    part_out[...] = jnp.sum(acc[...], axis=0, keepdims=True) * factor


def sweep(first, n_all, protos_all, x, lead, parts):
    width, n = x.shape
    return pl.pallas_call(
        functools.partial(sweep_kernel, first, float(n_all), float(protos_all), len(parts)),
        in_specs=[WHOLE] * (2 + len(parts)),
        out_specs=[WHOLE] * 3,
        out_shape=[
            jax.ShapeDtypeStruct((1, n), F32),
            jax.ShapeDtypeStruct((1, width), F32),
            jax.ShapeDtypeStruct((2, n), F32),
        ],
        scratch_shapes=[pltpu.VMEM((8, n), F32), pltpu.VMEM((16, n), F32)],
        compiler_params=params(8),
        cost_estimate=cost(4 * n * width, 2 * n * width),
        name="sweep",
    )(near(x), lead, *parts)


def weighted_student(weight, student, weighted):
    n, depth = student.shape
    for r in range(0, n, 128):
        s = student[r : r + 128, :].astype(F32).T * weight[:, r : r + 128]
        hi, lo = pieces(s, 2)
        weighted[:depth, r : r + 128] = hi
        weighted[depth:, r : r + 128] = lo


def soft_kernel(x, peak, lse, student, out, weighted):
    depth = student.shape[1]

    @pl.when(pl.program_id(0) == 0)
    def _():
        weighted_student(jnp.exp(peak[...] - lse[...]), student, weighted)

    g = lax.dot_general(x[...], weighted[...], NT, preferred_element_type=F32)
    out[...] = g[:, :depth] + g[:, depth:]


def soft_part(x, peak, lse, student):
    width, n = x.shape
    depth = student.shape[1]
    kb = min(512, width)
    return pl.pallas_call(
        soft_kernel,
        grid=(width // kb,),
        in_specs=[
            pl.BlockSpec((kb, n), lambda i: (i, 0)),
            full((1, n)),
            full((1, n)),
            full((n, depth)),
        ],
        out_specs=pl.BlockSpec((kb, depth), lambda i: (i, 0)),
        out_shape=jax.ShapeDtypeStruct((width, depth), F32),
        scratch_shapes=[pltpu.VMEM((2 * depth, n), BF16)],
        compiler_params=params(24),
        cost_estimate=cost(2 * n * width * depth, 2 * n * width),
        name="soft_part",
    )(far(x), peak, lse, student)


def grad_kernel(scale, x, factor, student, soft, col, *refs):
    ends, (out, weighted) = refs[:-2], refs[-2:]
    width = x.shape[0]
    depth = student.shape[1]
    n = x.shape[1]
    total = sum(e[:, :n] for e in ends)
    weighted_student(factor[...] / total, student, weighted)
    g = lax.dot_general(x[...], weighted[...], NT, preferred_element_type=F32)
    g = g[:, :depth] + g[:, depth:]
    for k in range(0, width, 128):
        a = soft[k : k + 128, :].T
        b = g[k : k + 128, :].T
        out[:, k : k + 128] = (scale * (a - b * col[:, k : k + 128])).astype(BF16)


def proto_grad_columns(scale, x, factor, student, soft, col, ends):
    width, n = x.shape
    depth = student.shape[1]
    return pl.pallas_call(
        functools.partial(grad_kernel, scale),
        in_specs=[WHOLE] * (5 + len(ends)),
        out_specs=WHOLE,
        out_shape=jax.ShapeDtypeStruct((depth, width), BF16),
        scratch_shapes=[pltpu.VMEM((2 * depth, n), BF16)],
        compiler_params=params(18),
        cost_estimate=cost(2 * n * width * depth, 2 * n * width),
        name="proto_grad",
    )(near(x), factor, student, soft, col, *ends)


def logit_kernel(protos_all, share, chunk, protos, teacher, student, glob_t, glob_s, *refs):
    ends = refs[:-8]
    grad_out, loss_out, lhs, rhs, grads, loss, in_sem, out_sem = refs[-8:]
    n = glob_t.shape[1]
    slots, rows, cb = grads.shape
    depth, width = protos.shape
    steps = width // cb

    def fetch(c):
        at = pl.ds(c * cb, cb)
        return pltpu.make_async_copy(protos.at[:, at], rhs.at[:depth, at], in_sem.at[c])

    def store(c, slot):
        at = pl.ds(pl.multiple_of(c * cb, cb), cb)
        return pltpu.make_async_copy(grads.at[slot], grad_out.at[:, at], out_sem.at[slot])

    for c in range(steps):
        fetch(c).start()

    lhs[:rows, :depth] = teacher[...]
    lhs[rows:, :depth] = student[...]
    me = lax.axis_index("dp")
    here = pl.ds(pl.multiple_of(me * rows, rows), rows)
    biases = (
        -jnp.log(sum(e[:, here] for e in ends)) - glob_t[:, here],
        math.log(protos_all) - glob_s[:, here],
    )
    lane = lax.broadcasted_iota(jnp.int32, (rows, 128), 1)
    for i, bias in enumerate(biases):
        b = jnp.broadcast_to(bias, (128, rows)).T
        ext = jnp.zeros((rows, 128), F32)
        for j, p in enumerate(pieces(b, 3)):
            ext = jnp.where(lane == j, p.astype(F32), ext)
        if i == 0:
            ext = jnp.where((lane >= 3) & (lane < 6), 1.0, ext)
        lhs[i * rows : (i + 1) * rows, depth:] = ext.astype(BF16)[:, :EXTRA]
    one = jnp.ones((1, share), F32)
    for d in range(width // share):
        e, j = divmod(d, len(ends))
        log_col = jnp.log(protos_all * ends[j][:, n + e * share : n + (e + 1) * share])
        to = pl.ds(pl.multiple_of((d ^ me) * share, share), share)
        rhs[depth:, to] = rows_of([one] * 3 + pieces(log_col, 3), EXTRA)
    loss[...] = jnp.zeros_like(loss)

    @pl.loop(0, steps)
    def _(c):
        slot = lax.rem(c, slots)

        @pl.when(c >= slots)
        def _():
            store(c - slots, slot).wait()

        pltpu.make_async_copy(
            protos.at[:, pl.ds(0, cb)], rhs.at[:depth, pl.ds(0, cb)], in_sem.at[c]
        ).wait()
        half = rows // 2
        for k in range(0, cb, chunk):
            at = pl.ds(pl.multiple_of(c * cb + k, chunk), chunk)
            for r in (0, half):
                here = slice(r, r + half)
                t = jnp.exp(jnp.dot(lhs[here, :], rhs[:, at], preferred_element_type=F32))
                u = jnp.dot(
                    lhs[rows + r : rows + r + half, :], rhs[:, at], preferred_element_type=F32
                )
                grads[slot, here, k : k + chunk] = (jnp.exp(u) - t).astype(BF16)
                p = t * u
                loss[here, :] += sum(p[:, j : j + 128] for j in range(0, chunk, 128))
        store(c, slot).start()

    for c in range(max(0, steps - slots), steps):
        store(c, c % slots).wait()
    loss_out[...] = jnp.sum(loss[...].T, axis=0, keepdims=True)


def logit_grads(protos_all, share, protos, teacher, student, glob_t, glob_s, ends):
    depth, width = protos.shape
    rows = teacher.shape[0]
    cb = min(4096, width)
    slots = min(4, width // cb)
    return pl.pallas_call(
        functools.partial(logit_kernel, float(protos_all), share, min(256, cb)),
        in_specs=[FAR] + [WHOLE] * (4 + len(ends)),
        out_specs=[FAR, WHOLE],
        out_shape=[
            pltpu.HBM((rows, width), BF16),
            jax.ShapeDtypeStruct((1, rows), F32),
        ],
        scratch_shapes=[
            pltpu.VMEM((2 * rows, depth + EXTRA), BF16),
            pltpu.VMEM((depth + EXTRA, width), BF16),
            pltpu.VMEM((slots, rows, cb), BF16),
            pltpu.VMEM((rows, 128), F32),
            pltpu.SemaphoreType.DMA((width // cb,)),
            pltpu.SemaphoreType.DMA((slots,)),
        ],
        compiler_params=params(58),
        cost_estimate=cost(
            4 * rows * width * depth, 2 * width * (rows + depth), 2 * rows * width
        ),
        name="logit_grads",
    )(far(protos), teacher, student, glob_t, glob_s, *ends)


def over_proto(v, combine):
    size = lax.axis_size("proto")
    if size == 2:
        return combine([v, lax.ppermute(v, "proto", [(0, 1), (1, 0)])])
    got = lax.all_gather(v, "proto")
    return combine([got[i] for i in range(size)])


def add(parts):
    return functools.reduce(jnp.add, parts)


def log_add(parts):
    peak = functools.reduce(jnp.maximum, parts)
    return peak + jnp.log(sum(jnp.exp(p - peak) for p in parts))


def dp_rounds():
    size = lax.axis_size("dp")
    rounds, bit = [], 1
    while bit < size:
        step = min(4, size // bit)
        rounds.append([s * bit for s in range(1, step)])
        bit *= step
    return rounds[::-1]


def swap(v, mask):
    size = lax.axis_size("dp")
    return lax.ppermute(v, "dp", [(a, a ^ mask) for a in range(size)])


def from_partners(v, masks):
    return [v] + [swap(v, m) for m in masks]


def radix4(v, combine, fill=None, args=()):
    rounds = dp_rounds()
    out = None
    if fill is not None:
        v, args = lax.optimization_barrier((v, args))
    for i, masks in enumerate(rounds):
        got = from_partners(v, masks)
        if i == 0 and fill is not None:
            got, out = lax.optimization_barrier((got, fill(*args)))
        if i == len(rounds) - 1:
            return got, out
        v = combine(got)


def in_dp_order(v):
    rest = v.shape[1:]
    size = lax.axis_size("dp")
    me = lax.axis_index("dp")
    bit = 1
    while bit < size:
        w = v.reshape((size // (2 * bit), 2, bit) + rest)
        w = jnp.where((me & bit) != 0, w[:, ::-1], w)
        v = w.reshape((size,) + rest)
        bit *= 2
    return v


def gather_round(v, masks):
    return jnp.stack(from_partners(v, masks), axis=1).reshape((-1,) + v.shape[1:])


def own_share(v):
    size = lax.axis_size("proto")
    rows = v.shape[0] // size
    return lax.dynamic_slice_in_dim(v, lax.axis_index("proto") * rows, rows, 0)


def both_shares(v):
    size = lax.axis_size("proto")
    if size == 2:
        other = lax.ppermute(v, "proto", [(0, 1), (1, 0)])
        mine = lax.axis_index("proto") == 0
        return jnp.concatenate([jnp.where(mine, v, other), jnp.where(mine, other, v)], axis=1)
    return lax.all_gather(v, "proto", axis=1, tiled=True)


def shards(teacher, student, prototypes):
    rows, depth = teacher.shape
    dp = lax.axis_size("dp")
    n = rows * dp
    protos_all = prototypes.shape[1] * lax.axis_size("proto")
    width = prototypes.shape[1] // dp

    own = lax.all_to_all(prototypes, "dp", 1, 0, tiled=True)
    crops = jnp.stack([own_share(teacher), own_share(student)])[None]
    rounds = dp_rounds()
    for masks in rounds[:-1]:
        crops = gather_round(crops, masks)
    own, crops, prototypes = lax.optimization_barrier((own, crops, prototypes))
    gathered = lax.all_gather(prototypes, "dp", axis=0, tiled=True)
    teacher_all, student_all = [
        both_shares(in_dp_order(gather_round(crops[:, i], rounds[-1]))).reshape(n, depth)
        for i in range(2)
    ]

    x_t, peak_t, lse_t = exp_rows(own, teacher_all, True)
    lses, (x_s, peak_s, lse_s) = radix4(
        over_proto(lse_t, log_add),
        log_add,
        lambda crops: exp_rows(own, crops, False),
        (student_all,),
    )
    part, col, lead = sweep(True, n, protos_all, x_t, peak_t, lses)
    factor, glob_t = lead[:1], lead[1:]

    def mixed(parts):
        return jnp.concatenate([add([p[:1] for p in parts]), log_add([p[1:] for p in parts])])

    soft = None
    for it in range(1, ITERS):
        part = over_proto(part, add)
        if it == 1:
            got, _ = radix4(jnp.concatenate([part, over_proto(lse_s, log_add)]), mixed)
            glob_s = log_add([p[1:] for p in got])
            got = [p[:1] for p in got]
        else:
            got, soft = radix4(
                part,
                add,
                lambda peak: soft_part(x_s, peak, glob_s, student_all),
                (peak_s,),
            )
        part, col, _ = sweep(False, n, protos_all, x_t, factor, got)

    ends = [jnp.concatenate([over_proto(part, add), col], axis=1)]
    for masks in dp_rounds():
        if len(ends) > 1:
            total = add([e[:, :n] for e in ends])
            cols = jnp.stack([e[:, n:].reshape(-1, width) for e in ends], axis=1)
            ends = [jnp.concatenate([total, cols.reshape(1, -1)], axis=1)]
        ends = from_partners(ends[0], masks)

    grad = proto_grad_columns(protos_all / 128.0, x_t, factor, student_all, soft, col, ends)
    proto_grad = lax.all_to_all(grad, "dp", 0, 1, tiled=True)

    logit_grad, loss = logit_grads(
        protos_all, width, gathered, teacher, student, glob_t, glob_s, ends
    )
    crop_loss = math.log(protos_all) - over_proto(loss[0], add) / protos_all
    return crop_loss, logit_grad, proto_grad


def solution(mesh):
    placed = (P("dp", None), P("dp", None), P("dp", "proto"))
    return jax.shard_map(
        shards,
        mesh=mesh,
        in_specs=placed,
        out_specs=(P("dp"), P("dp", "proto"), P("dp", "proto")),
        check_vma=False,
    )
```

```python
import functools
import math

import jax
import jax.numpy as jnp
from jax import lax
from jax.experimental import pallas as pl
from jax.experimental.pallas import tpu as pltpu
from jax.sharding import PartitionSpec as P

ITERS = 3
F32 = jnp.float32
BF16 = jnp.bfloat16
NT = (((1,), (1,)), ((), ()))
EXTRA = 16
WHOLE = pl.BlockSpec(memory_space=pltpu.VMEM)
FAR = pl.BlockSpec(memory_space=pltpu.HBM)


def params(mib):
    return pltpu.CompilerParams(vmem_limit_bytes=mib * 1024 * 1024)


def cost(flops, nbytes, exps=0):
    return pl.CostEstimate(flops=flops, bytes_accessed=nbytes, transcendentals=exps)


def near(x):
    return pltpu.with_memory_space_constraint(x, pltpu.VMEM)


def far(x):
    return pltpu.with_memory_space_constraint(x, pltpu.HBM)


def full(shape):
    return pl.BlockSpec(shape, lambda i: (0,) * len(shape))


def pieces(v, count):
    out = []
    for _ in range(count):
        p = v.astype(BF16)
        out.append(p)
        v = v - p.astype(F32)
    return out


def rows_of(parts, height):
    n = parts[0].shape[1]
    row = lax.broadcasted_iota(jnp.int32, (height, n), 0)
    block = jnp.zeros((height, n), F32)
    for i, p in enumerate(parts):
        block = jnp.where(row == i, jnp.broadcast_to(p.astype(F32), (height, n)), block)
    return block.astype(BF16)


def exp_kernel(
    rb, kc, resident, protos, crops, x, peak_out, lse_out, protos_t, scores_a, scores_b, *refs
):
    width, n = x.shape
    blocks = n // rb
    for q in range(0, width, 128):
        protos_t[q : q + 128, :] = protos[:, q : q + 128].astype(F32).T.astype(BF16)

    def at(b):
        return pl.ds(b * rb if isinstance(b, int) else pl.multiple_of(b * rb, rb), rb)

    def leave(b, slot):
        return pltpu.make_async_copy(refs[0].at[slot], x.at[:, at(b)], refs[1].at[slot])

    def stage(new, new_scores, old, old_scores, peak, slot=0):
        new_peak = jnp.full((8, rb), -jnp.inf, F32)
        total = jnp.zeros((8, rb), F32)
        for q in range(0, width, kc):
            if new is not None:
                s = lax.dot_general(
                    protos_t[q : q + kc, :], crops[at(new), :], NT, preferred_element_type=F32
                )
                new_scores[q : q + kc, :] = s
                new_peak = jnp.maximum(new_peak, jnp.max(s.reshape(kc // 8, 8, rb), axis=0))
            if old is not None:
                e = jnp.exp(old_scores[q : q + kc, :] - peak)
                total = total + jnp.sum(e.reshape(kc // 8, 8, rb), axis=0)
                if resident:
                    x[q : q + kc, at(old)] = e.astype(BF16)
                else:
                    refs[0][slot, q : q + kc, :] = e.astype(BF16)
        if old is not None:
            peak_out[:, at(old)] = peak
            lse_out[:, at(old)] = peak + jnp.log(jnp.sum(total, axis=0, keepdims=True))
            if not resident:
                leave(old, slot).start()
        return jnp.max(new_peak, axis=0, keepdims=True)

    def free(j, slot):
        if not resident and not (isinstance(j, int) and j == 0):

            @pl.when(j > 0)
            def _():
                leave(2 * j - 2 + slot, slot).wait()

    def two(j, peak):
        free(j, 0)
        peak = stage(2 * j + 1, scores_b, 2 * j, scores_a, peak, 0)
        free(j, 1)
        return stage(2 * j + 2, scores_a, 2 * j + 1, scores_b, peak, 1)

    last = blocks // 2 - 1
    peak = lax.fori_loop(0, last, two, stage(0, scores_a, None, None, None))
    free(last, 0)
    peak = stage(blocks - 1, scores_b, blocks - 2, scores_a, peak, 0)
    free(last, 1)
    stage(None, None, blocks - 1, scores_b, peak, 1)
    if not resident:
        leave(blocks - 2, 0).wait()
        leave(blocks - 1, 1).wait()


def exp_rows(protos, crops, resident):
    depth, width = protos.shape
    n = crops.shape[0]
    rb = 512
    leaving = [pltpu.VMEM((2, width, rb), BF16), pltpu.SemaphoreType.DMA((2,))]
    return pl.pallas_call(
        functools.partial(exp_kernel, rb, 128, resident),
        in_specs=[WHOLE, WHOLE],
        out_specs=[WHOLE if resident else FAR, WHOLE, WHOLE],
        out_shape=[
            (pltpu.VMEM if resident else pltpu.HBM)((width, n), BF16),
            jax.ShapeDtypeStruct((1, n), F32),
            jax.ShapeDtypeStruct((1, n), F32),
        ],
        scratch_shapes=[
            pltpu.VMEM((width, depth), BF16),
            pltpu.VMEM((width, rb), F32),
            pltpu.VMEM((width, rb), F32),
        ]
        + ([] if resident else leaving),
        compiler_params=params(18 if resident else 22),
        cost_estimate=cost(2 * n * width * depth, 2 * n * width, n * width),
        name="exp_rows",
    )(protos, crops)


def sweep_kernel(first, n_all, protos_all, count, x, lead, *refs):
    parts, (part_out, col_out, lead_out, weights, acc) = refs[:count], refs[count:]
    width, n = x.shape
    if first:
        peak = functools.reduce(
            jnp.maximum, [jnp.max(p[...], axis=0, keepdims=True) for p in parts]
        )
        total = sum(jnp.sum(jnp.exp(p[...] - peak), axis=0, keepdims=True) for p in parts)
        lse = peak + jnp.log(total)
        factor = jnp.exp(lead[...] - lse)
        weight = factor
        lead_out[0:1, :] = factor
        lead_out[1:2, :] = lse
    else:
        factor = lead[...]
        total = sum(jnp.sum(p[...], axis=0, keepdims=True) for p in parts)
        weight = factor / (n_all * total)
    weights[...] = jnp.broadcast_to(weight, weights.shape)
    acc[...] = jnp.zeros_like(acc)
    kb = min(512, width)
    row = lax.broadcasted_iota(jnp.int32, (16, kb), 0)

    def scales(q):
        sums = jnp.zeros((kb // 8, 8, 128), F32)
        for r in range(0, n, 128):
            v = x[pl.ds(q, kb), r : r + 128].astype(F32)
            sums = sums + v.reshape(kb // 8, 8, 128) * weights[:, r : r + 128][None]
        sums = sums.reshape(kb, 128)
        sums = [jnp.sum(sums[i : i + 128].T, axis=0, keepdims=True) for i in range(0, kb, 128)]
        return 1.0 / (protos_all * jnp.concatenate(sums, axis=1))

    def totals(q, col):
        col_out[:, pl.ds(q, kb)] = col
        hi = col.astype(BF16).astype(F32)
        rows = jnp.where(row == 0, hi, jnp.where(row == 1, col - hi, 0.0)).astype(BF16)
        acc[...] += jnp.dot(rows, x[pl.ds(q, kb), :], preferred_element_type=F32)

    def both(i, col):
        q = pl.multiple_of(i * kb, kb)
        later = scales(pl.multiple_of(q + kb, kb))
        totals(q, col)
        return later

    totals(width - kb, lax.fori_loop(0, width // kb - 1, both, scales(0)))
    part_out[...] = jnp.sum(acc[...], axis=0, keepdims=True) * factor


def sweep(first, n_all, protos_all, x, lead, parts):
    width, n = x.shape
    return pl.pallas_call(
        functools.partial(sweep_kernel, first, float(n_all), float(protos_all), len(parts)),
        in_specs=[WHOLE] * (2 + len(parts)),
        out_specs=[WHOLE] * 3,
        out_shape=[
            jax.ShapeDtypeStruct((1, n), F32),
            jax.ShapeDtypeStruct((1, width), F32),
            jax.ShapeDtypeStruct((2, n), F32),
        ],
        scratch_shapes=[pltpu.VMEM((8, n), F32), pltpu.VMEM((16, n), F32)],
        compiler_params=params(8),
        cost_estimate=cost(4 * n * width, 2 * n * width),
        name="sweep",
    )(near(x), lead, *parts)


def weighted_student(weight, student, weighted):
    n, depth = student.shape
    for r in range(0, n, 128):
        s = student[r : r + 128, :].astype(F32).T * weight[:, r : r + 128]
        hi, lo = pieces(s, 2)
        weighted[:depth, r : r + 128] = hi
        weighted[depth:, r : r + 128] = lo


def soft_kernel(x, peak, lse, student, out, weighted):
    depth = student.shape[1]

    @pl.when(pl.program_id(0) == 0)
    def _():
        weighted_student(jnp.exp(peak[...] - lse[...]), student, weighted)

    g = lax.dot_general(x[...], weighted[...], NT, preferred_element_type=F32)
    out[...] = g[:, :depth] + g[:, depth:]


def soft_part(x, peak, lse, student):
    width, n = x.shape
    depth = student.shape[1]
    kb = min(512, width)
    return pl.pallas_call(
        soft_kernel,
        grid=(width // kb,),
        in_specs=[
            pl.BlockSpec((kb, n), lambda i: (i, 0)),
            full((1, n)),
            full((1, n)),
            full((n, depth)),
        ],
        out_specs=pl.BlockSpec((kb, depth), lambda i: (i, 0)),
        out_shape=jax.ShapeDtypeStruct((width, depth), F32),
        scratch_shapes=[pltpu.VMEM((2 * depth, n), BF16)],
        compiler_params=params(24),
        cost_estimate=cost(2 * n * width * depth, 2 * n * width),
        name="soft_part",
    )(far(x), peak, lse, student)


def grad_kernel(scale, x, factor, student, soft, col, *refs):
    ends, (out, weighted) = refs[:-2], refs[-2:]
    width = x.shape[0]
    depth = student.shape[1]
    n = x.shape[1]
    total = sum(e[:, :n] for e in ends)
    weighted_student(factor[...] / total, student, weighted)
    g = lax.dot_general(x[...], weighted[...], NT, preferred_element_type=F32)
    g = g[:, :depth] + g[:, depth:]
    for k in range(0, width, 128):
        a = soft[k : k + 128, :].T
        b = g[k : k + 128, :].T
        out[:, k : k + 128] = (scale * (a - b * col[:, k : k + 128])).astype(BF16)


def proto_grad_columns(scale, x, factor, student, soft, col, ends):
    width, n = x.shape
    depth = student.shape[1]
    return pl.pallas_call(
        functools.partial(grad_kernel, scale),
        in_specs=[WHOLE] * (5 + len(ends)),
        out_specs=WHOLE,
        out_shape=jax.ShapeDtypeStruct((depth, width), BF16),
        scratch_shapes=[pltpu.VMEM((2 * depth, n), BF16)],
        compiler_params=params(18),
        cost_estimate=cost(2 * n * width * depth, 2 * n * width),
        name="proto_grad",
    )(near(x), factor, student, soft, col, *ends)


def logit_kernel(protos_all, share, chunk, protos, teacher, student, glob_t, glob_s, *refs):
    ends = refs[:-8]
    grad_out, loss_out, lhs, rhs, grads, loss, in_sem, out_sem = refs[-8:]
    n = glob_t.shape[1]
    slots, rows, cb = grads.shape
    depth, width = protos.shape
    steps = width // cb

    def fetch(c):
        at = pl.ds(c * cb, cb)
        return pltpu.make_async_copy(protos.at[:, at], rhs.at[:depth, at], in_sem.at[c])

    def store(c, slot):
        at = pl.ds(pl.multiple_of(c * cb, cb), cb)
        return pltpu.make_async_copy(grads.at[slot], grad_out.at[:, at], out_sem.at[slot])

    for c in range(steps):
        fetch(c).start()

    lhs[:rows, :depth] = teacher[...]
    lhs[rows:, :depth] = student[...]
    me = lax.axis_index("dp")
    here = pl.ds(pl.multiple_of(me * rows, rows), rows)
    biases = (
        -jnp.log(sum(e[:, here] for e in ends)) - glob_t[:, here],
        math.log(protos_all) - glob_s[:, here],
    )
    lane = lax.broadcasted_iota(jnp.int32, (rows, 128), 1)
    for i, bias in enumerate(biases):
        b = jnp.broadcast_to(bias, (128, rows)).T
        ext = jnp.zeros((rows, 128), F32)
        for j, p in enumerate(pieces(b, 3)):
            ext = jnp.where(lane == j, p.astype(F32), ext)
        if i == 0:
            ext = jnp.where((lane >= 3) & (lane < 6), 1.0, ext)
        lhs[i * rows : (i + 1) * rows, depth:] = ext.astype(BF16)[:, :EXTRA]
    one = jnp.ones((1, share), F32)
    for d in range(width // share):
        e, j = divmod(d, len(ends))
        log_col = jnp.log(protos_all * ends[j][:, n + e * share : n + (e + 1) * share])
        to = pl.ds(pl.multiple_of((d ^ me) * share, share), share)
        rhs[depth:, to] = rows_of([one] * 3 + pieces(log_col, 3), EXTRA)
    loss[...] = jnp.zeros_like(loss)

    @pl.loop(0, steps)
    def _(c):
        slot = lax.rem(c, slots)

        @pl.when(c >= slots)
        def _():
            store(c - slots, slot).wait()

        pltpu.make_async_copy(
            protos.at[:, pl.ds(0, cb)], rhs.at[:depth, pl.ds(0, cb)], in_sem.at[c]
        ).wait()
        half = rows // 2
        for k in range(0, cb, chunk):
            at = pl.ds(pl.multiple_of(c * cb + k, chunk), chunk)
            for r in (0, half):
                here = slice(r, r + half)
                t = jnp.exp(jnp.dot(lhs[here, :], rhs[:, at], preferred_element_type=F32))
                u = jnp.dot(
                    lhs[rows + r : rows + r + half, :], rhs[:, at], preferred_element_type=F32
                )
                grads[slot, here, k : k + chunk] = (jnp.exp(u) - t).astype(BF16)
                p = t * u
                loss[here, :] += sum(p[:, j : j + 128] for j in range(0, chunk, 128))
        store(c, slot).start()

    for c in range(max(0, steps - slots), steps):
        store(c, c % slots).wait()
    loss_out[...] = jnp.sum(loss[...].T, axis=0, keepdims=True)


def logit_grads(protos_all, share, protos, teacher, student, glob_t, glob_s, ends):
    depth, width = protos.shape
    rows = teacher.shape[0]
    cb = min(4096, width)
    slots = min(4, width // cb)
    return pl.pallas_call(
        functools.partial(logit_kernel, float(protos_all), share, min(256, cb)),
        in_specs=[FAR] + [WHOLE] * (4 + len(ends)),
        out_specs=[FAR, WHOLE],
        out_shape=[
            pltpu.HBM((rows, width), BF16),
            jax.ShapeDtypeStruct((1, rows), F32),
        ],
        scratch_shapes=[
            pltpu.VMEM((2 * rows, depth + EXTRA), BF16),
            pltpu.VMEM((depth + EXTRA, width), BF16),
            pltpu.VMEM((slots, rows, cb), BF16),
            pltpu.VMEM((rows, 128), F32),
            pltpu.SemaphoreType.DMA((width // cb,)),
            pltpu.SemaphoreType.DMA((slots,)),
        ],
        compiler_params=params(58),
        cost_estimate=cost(
            4 * rows * width * depth, 2 * width * (rows + depth), 2 * rows * width
        ),
        name="logit_grads",
    )(far(protos), teacher, student, glob_t, glob_s, *ends)


def over_proto(v, combine):
    size = lax.axis_size("proto")
    if size == 2:
        return combine([v, lax.ppermute(v, "proto", [(0, 1), (1, 0)])])
    got = lax.all_gather(v, "proto")
    return combine([got[i] for i in range(size)])


def add(parts):
    return functools.reduce(jnp.add, parts)


def log_add(parts):
    peak = functools.reduce(jnp.maximum, parts)
    return peak + jnp.log(sum(jnp.exp(p - peak) for p in parts))


def dp_rounds():
    size = lax.axis_size("dp")
    rounds, bit = [], 1
    while bit < size:
        step = min(4, size // bit)
        rounds.append([s * bit for s in range(1, step)])
        bit *= step
    return rounds[::-1]


def swap(v, mask):
    size = lax.axis_size("dp")
    return lax.ppermute(v, "dp", [(a, a ^ mask) for a in range(size)])


def from_partners(v, masks):
    return [v] + [swap(v, m) for m in masks]


def radix4(v, combine, fill=None, args=()):
    rounds = dp_rounds()
    out = None
    if fill is not None:
        v, args = lax.optimization_barrier((v, args))
    for i, masks in enumerate(rounds):
        got = from_partners(v, masks)
        if i == 0 and fill is not None:
            got, out = lax.optimization_barrier((got, fill(*args)))
        if i == len(rounds) - 1:
            return got, out
        v = combine(got)


def in_dp_order(v):
    rest = v.shape[1:]
    size = lax.axis_size("dp")
    me = lax.axis_index("dp")
    bit = 1
    while bit < size:
        w = v.reshape((size // (2 * bit), 2, bit) + rest)
        w = jnp.where((me & bit) != 0, w[:, ::-1], w)
        v = w.reshape((size,) + rest)
        bit *= 2
    return v


def gather_round(v, masks):
    return jnp.stack(from_partners(v, masks), axis=1).reshape((-1,) + v.shape[1:])


def own_share(v):
    size = lax.axis_size("proto")
    rows = v.shape[0] // size
    return lax.dynamic_slice_in_dim(v, lax.axis_index("proto") * rows, rows, 0)


def both_shares(v):
    size = lax.axis_size("proto")
    if size == 2:
        other = lax.ppermute(v, "proto", [(0, 1), (1, 0)])
        mine = lax.axis_index("proto") == 0
        return jnp.concatenate([jnp.where(mine, v, other), jnp.where(mine, other, v)], axis=1)
    return lax.all_gather(v, "proto", axis=1, tiled=True)


def shards(teacher, student, prototypes):
    rows, depth = teacher.shape
    dp = lax.axis_size("dp")
    n = rows * dp
    protos_all = prototypes.shape[1] * lax.axis_size("proto")
    width = prototypes.shape[1] // dp

    crops = jnp.stack([own_share(teacher), own_share(student)])[None]
    rounds = dp_rounds()
    got = from_partners(crops, rounds[0])
    mine, got[1] = lax.optimization_barrier((prototypes, got[1]))
    own = lax.all_to_all(mine, "dp", 1, 0, tiled=True)
    crops = jnp.stack(got, axis=1).reshape((-1,) + crops.shape[1:])
    for masks in rounds[1:-1]:
        crops = gather_round(crops, masks)
    own, prototypes = lax.optimization_barrier((own, prototypes))
    gathered = lax.all_gather(prototypes, "dp", axis=0, tiled=True)
    teacher_all, student_all = [
        both_shares(in_dp_order(gather_round(crops[:, i], rounds[-1]))).reshape(n, depth)
        for i in range(2)
    ]

    x_t, peak_t, lse_t = exp_rows(own, teacher_all, True)
    lses, (x_s, peak_s, lse_s) = radix4(
        over_proto(lse_t, log_add),
        log_add,
        lambda crops: exp_rows(own, crops, False),
        (student_all,),
    )
    part, col, lead = sweep(True, n, protos_all, x_t, peak_t, lses)
    factor, glob_t = lead[:1], lead[1:]

    def mixed(parts):
        return jnp.concatenate([add([p[:1] for p in parts]), log_add([p[1:] for p in parts])])

    soft = None
    for it in range(1, ITERS):
        part = over_proto(part, add)
        if it == 1:
            got, _ = radix4(jnp.concatenate([part, over_proto(lse_s, log_add)]), mixed)
            glob_s = log_add([p[1:] for p in got])
            got = [p[:1] for p in got]
        else:
            got, soft = radix4(
                part,
                add,
                lambda peak: soft_part(x_s, peak, glob_s, student_all),
                (peak_s,),
            )
        part, col, _ = sweep(False, n, protos_all, x_t, factor, got)

    ends = [jnp.concatenate([over_proto(part, add), col], axis=1)]
    for masks in dp_rounds():
        if len(ends) > 1:
            total = add([e[:, :n] for e in ends])
            cols = jnp.stack([e[:, n:].reshape(-1, width) for e in ends], axis=1)
            ends = [jnp.concatenate([total, cols.reshape(1, -1)], axis=1)]
        ends = from_partners(ends[0], masks)

    grad = proto_grad_columns(protos_all / 128.0, x_t, factor, student_all, soft, col, ends)
    proto_grad = lax.all_to_all(grad, "dp", 0, 1, tiled=True)

    logit_grad, loss = logit_grads(
        protos_all, width, gathered, teacher, student, glob_t, glob_s, ends
    )
    crop_loss = math.log(protos_all) - over_proto(loss[0], add) / protos_all
    return crop_loss, logit_grad, proto_grad


def solution(mesh):
    placed = (P("dp", None), P("dp", None), P("dp", "proto"))
    return jax.shard_map(
        shards,
        mesh=mesh,
        in_specs=placed,
        out_specs=(P("dp"), P("dp", "proto"), P("dp", "proto")),
        check_vma=False,
    )
```
